256 devices in a mesh: replica: 8 (over x, y_hi), fsdp: 32 (over y_lo, z, core).
Axes of the slice: x: 4, y: 4 (y_hi: 2, y_lo: 2; y = y_hi * 2 + y_lo), z: 8, core: 2. Of those that a mesh axis runs over, the one named last changes fastest.
Arguments:
- inner: bfloat16 [8, 256, 28672], P('replica', 'fsdp'), may hold values from -6 to 6
- outer: float32 [256, 28672], P('fsdp'), may hold values from -6 to 6
- momentum: float32 [256, 28672], P('fsdp', 'replica'), may hold values from -4 to 4
Outputs:
- outer_new: float32 [256, 28672], P('fsdp')
- momentum_new: float32 [256, 28672], P('fsdp', 'replica')
- gathered: bfloat16 [8, 256, 28672], P('replica')
The draws below stay inside these ranges and needn't reach their ends.
All inputs are finite; a program needn't handle non-finite values.
Results may differ from the reference program's by a relative error of at most 0.0004.
Values may be sent and summed in bfloat16 or wider, within the bound.
No kernel may reach another device: no remote copies, remote signals or barrier semaphores. Data moves between devices by JAX's collectives and lax.ppermute only.
A program may use at most 128 MiB of HBM per device.

```python
import jax
import jax.numpy as jnp

FF = 28672
ROWS = 256
REPLICAS = 8
N_REPLICA = 8


def level_of(stream_key, shape, shards, smallest, largest):
    factor_of, own = 1.0, jax.random.fold_in(stream_key, 6)
    for axis_at, parts in shards:
        steps = jnp.exp(jax.random.uniform(jax.random.fold_in(own, axis_at), (parts,), jnp.float32, smallest / len(shards), largest / len(shards)))
        factor_of = factor_of * jnp.repeat(steps, shape[axis_at] // parts).reshape([-1 if axis == axis_at else 1 for axis in range(len(shape))])
    return factor_of


def centred(own_key, shape, spread, bound, cuts=(), held_as=jnp.bfloat16):
    array = spread * jax.random.normal(own_key, shape, jnp.float32)
    if cuts:
        array = array * level_of(own_key, shape, cuts, -0.22, 0.18)
    return jnp.clip(array, -bound, bound).astype(held_as)


def setup_inputs(seed: int = 0) -> dict:
    keys = jax.random.split(jax.random.key(seed), 4)
    inner = centred(keys[0], (REPLICAS, ROWS, FF), 1.0, 6.0, ((0, 8), (1, 32)))
    outer = centred(keys[1], (ROWS, FF), 1.0, 6.0, ((0, 32),), jnp.float32)
    momentum = centred(keys[2], (ROWS, FF), 0.5, 4.0, ((0, 32), (1, 8)), jnp.float32)
    return dict(inner=inner, outer=outer, momentum=momentum)


def reference(inner, outer, momentum):
    delta = outer[None] - inner.astype(jnp.float32)
    average = jnp.sum(delta, axis=0) / N_REPLICA
    momentum_new = 0.9 * momentum + average
    outer_new = outer - 0.7 * (average + 0.9 * momentum_new)
    blended = (0.5 * inner.astype(jnp.float32) + 0.5 * outer_new[None]).astype(jnp.bfloat16)
    return outer_new, momentum_new, blended
```

```python
import jax
import jax.numpy as jnp
from jax import lax
from jax.experimental import pallas as pl
from jax.experimental.pallas import tpu as pltpu
from jax.sharding import PartitionSpec as P

REPLICAS = 8
RUNS, SLOTS, CORES = 2, 8, 2
TILE = (8, 128)
SPLIT = 13


def coords(index):
    return index // (SLOTS * CORES), index // CORES % SLOTS, index % CORES


def fsdp_index(run, slot, core):
    return (run % RUNS * SLOTS + slot % SLOTS) * CORES + core % CORES


def move(array, target):
    return lax.ppermute(array, "fsdp", [(i, fsdp_index(*target(*coords(i)))) for i in range(RUNS * SLOTS * CORES)])


def swap_run(array):
    return move(array, lambda run, slot, core: (run + 1, slot, core))


def swap_core(array):
    return move(array, lambda run, slot, core: (run, slot, core + 1))


def along_slots(array):
    return move(array, lambda run, slot, core: (run, slot + (1 if core == 0 else -1), core))


def swap_replica(array, bits):
    return lax.ppermute(array, "replica", [(i, i ^ bits) for i in range(REPLICAS)])


def by_xor(array, index):
    count = array.shape[0]
    levels = count.bit_length() - 1
    rest = array.shape[1:]
    array = array.reshape((2,) * levels + rest)
    for level in range(levels):
        bit = (index >> (levels - 1 - level)) & 1
        array = jnp.where(bit == 1, jnp.flip(array, level), array)
    return array.reshape((count,) + rest)


def place(out, groups, shape, carried=None):
    arrays = [array for array, *_ in groups]
    through = ([] if out is None else [out]) + ([] if carried is None else [carried])
    blocks = [
        (at, lead, where, first, tiles)
        for at, (_, targets, first, tiles) in enumerate(groups)
        for lead, where in enumerate(targets)
    ]

    def kernel(*refs):
        held, result, sems = refs[: len(arrays)], refs[len(arrays) + len(through)], refs[-1]
        own_run, own_slot, own_core = coords(lax.axis_index("fsdp"))
        copies = []
        for number, (at, lead, (run, hops, core, came), first, tiles) in enumerate(blocks):
            receiver = (own_core + came) % CORES
            block = fsdp_index(own_run + run, own_slot + (2 * receiver - 1) * hops, receiver + core)
            copies.append(
                pltpu.make_async_copy(held[at].at[lead], result.at[block, :, pl.ds(first, tiles)], sems.at[number])
            )
        for copy in copies:
            copy.start()
        for copy in copies:
            copy.wait()

    anywhere = pl.BlockSpec(memory_space=pl.ANY)
    moved = sum(array.size * array.dtype.itemsize for array in arrays)
    results = [jax.ShapeDtypeStruct(shape, jnp.bfloat16)]
    results += [] if carried is None else [jax.ShapeDtypeStruct(carried.shape, carried.dtype)]
    aliases = {len(arrays) + at: at + (out is None) for at in range(len(through))}
    done = pl.pallas_call(
        kernel,
        out_shape=results,
        in_specs=[pl.BlockSpec(memory_space=pltpu.VMEM)] * len(arrays) + [anywhere] * len(through),
        out_specs=[anywhere] * len(results),
        scratch_shapes=[pltpu.SemaphoreType.DMA((len(blocks),))],
        input_output_aliases=aliases,
        compiler_params=pltpu.CompilerParams(vmem_limit_bytes=moved + (1 << 20)),
        cost_estimate=pl.CostEstimate(flops=0, bytes_accessed=2 * moved, transcendentals=0),
    )(*arrays, *through)
    return done[0] if carried is None else done


def step(inner, outer, momentum):
    terms = lax.all_to_all(inner, "replica", 0, 0).astype(jnp.float32)
    average = outer - jnp.sum(terms, axis=0) / REPLICAS
    momentum_new = 0.9 * momentum + average
    outer_new = outer - 0.7 * (average + 0.9 * momentum_new)
    blended = (0.5 * terms + 0.5 * outer_new).astype(jnp.bfloat16)
    return outer_new, momentum_new, lax.all_to_all(blended, "replica", 0, 0)


def gather(split, joined, shape):
    (alone, first_a), (both, first_b) = split, joined
    count_a, count_b = alone.shape[1], both.shape[1]

    def blocks_a(array, hops, came, run=0):
        targets = [(run, hop, core, came) for hop, kinds in hops for core in range(kinds)]
        return array, targets, first_a, count_a

    def blocks_b(array, hops, came):
        targets = [(at % RUNS, hops, at // RUNS, came) for at in range(array.shape[0])]
        return array, targets, first_b, count_b

    alone, both = alone[None], both[None]
    beside = swap_run(both)
    pair = jnp.concatenate([alone, swap_core(alone)])
    y0 = swap_run(alone)
    quad = jnp.concatenate([both, beside])
    quad = jnp.concatenate([quad, swap_core(quad)])
    a, b = along_slots(pair), along_slots(quad)
    cy = swap_core(y0)
    ready = [blocks_a(pair, [(0, 2)], 0), blocks_b(quad, 0, 0)]
    later = [blocks_a(y0, [(0, 1)], 0, 1), blocks_a(cy, [(0, 1)], 1, 1)]
    out = None
    for hops in range(1, SLOTS // 2 + 1):
        kinds = 2 if hops < SLOTS // 2 - 1 else 1
        last = hops == SLOTS // 2
        out, a = place(out, ready, shape, a)
        next_a = None if last else along_slots(a[:kinds])
        held = [(hops, a.shape[0])]
        y, ca = swap_run(a), swap_core(a)
        cy = swap_core(y)
        ready = later + [blocks_a(a, held, 0)]
        later = [blocks_a(y, held, 0, 1), blocks_a(cy, held, 1, 1), blocks_a(ca, held, 1)]
        out, b = place(out, ready, shape, b)
        next_b = None if last else along_slots(b[: RUNS * kinds])
        cb = swap_core(b)
        ready = [blocks_b(b, hops, 0)]
        later += [blocks_b(cb, hops, 1)]
        a, b = next_a, next_b
    return place(out, ready + later, shape)


def body(inner, outer, momentum):
    width = momentum.shape[1] // TILE[1]
    replica = lax.axis_index("replica")

    def tiles(array):
        array = array.reshape(TILE[0], -1, width, TILE[1])
        return array.transpose(1, 2, 0, 3)

    def rows(array):
        return array.transpose(2, 0, 1, 3).reshape(TILE[0], -1)

    inner, outer, momentum = tiles(inner[0]), tiles(outer), tiles(momentum)[0]
    own_outer = lax.dynamic_index_in_dim(outer, replica, 0, keepdims=False)
    shape = (RUNS * SLOTS * CORES, REPLICAS, width) + TILE

    outer_new, momentum_new, blended = step(inner, own_outer, momentum)
    out = gather((blended[:, :SPLIT], 0), (blended[:, SPLIT:], SPLIT), shape)

    pair = by_xor(jnp.stack([outer_new, swap_replica(outer_new, 1)]), replica & 1)
    four = jnp.stack([pair] + [swap_replica(pair, 2 * bits) for bits in range(1, 4)])
    outer_all = by_xor(four, replica >> 1).reshape((REPLICAS,) + outer_new.shape)

    gathered = out.transpose(0, 3, 1, 2, 4).reshape(1, -1, REPLICAS * width * TILE[1])
    return rows(outer_all), rows(momentum_new[None]), gathered


def solution(mesh):
    placed = (P("replica", "fsdp", None), P("fsdp", None), P("fsdp", "replica"))
    return jax.shard_map(
        body,
        mesh=mesh,
        in_specs=placed,
        out_specs=(P("fsdp", None), P("fsdp", "replica"), P("replica", None, None)),
        check_vma=False,
    )
```

```python
import jax
import jax.numpy as jnp
from jax import lax
from jax.experimental import pallas as pl
from jax.experimental.pallas import tpu as pltpu
from jax.sharding import PartitionSpec as P

REPLICAS = 8
RUNS, SLOTS, CORES = 2, 8, 2
TILE = (8, 128)
GATE_FLOPS, PLACE_FLOPS = 6_000_000_000, 2_000_000_000
SPLIT = 14


def coords(index):
    return index // (SLOTS * CORES), index // CORES % SLOTS, index % CORES


def fsdp_index(run, slot, core):
    return (run % RUNS * SLOTS + slot % SLOTS) * CORES + core % CORES


def move(array, target):
    return lax.ppermute(array, "fsdp", [(i, fsdp_index(*target(*coords(i)))) for i in range(RUNS * SLOTS * CORES)])


def swap_run(array):
    return move(array, lambda run, slot, core: (run + 1, slot, core))


def swap_core(array):
    return move(array, lambda run, slot, core: (run, slot, core + 1))


def along_slots(array):
    return move(array, lambda run, slot, core: (run, slot + (1 if core == 0 else -1), core))


def place(out, groups, shape):
    arrays = [array for array, *_ in groups]
    through = [] if out is None else [out]
    blocks = [
        (at, lead, where, first, tiles)
        for at, (_, targets, first, tiles) in enumerate(groups)
        for lead, where in enumerate(targets)
    ]

    def kernel(*refs):
        held, result, sems = refs[: len(arrays)], refs[-2], refs[-1]
        own_run, own_slot, own_core = coords(lax.axis_index("fsdp"))
        copies = []
        for number, (at, lead, (run, hops, core, came), first, tiles) in enumerate(blocks):
            receiver = (own_core + came) % CORES
            block = fsdp_index(own_run + run, own_slot + (2 * receiver - 1) * hops, receiver + core)
            copies.append(
                pltpu.make_async_copy(held[at].at[lead], result.at[block, :, pl.ds(first, tiles)], sems.at[number])
            )
        for copy in copies:
            copy.start()
        for copy in copies:
            copy.wait()

    anywhere = pl.BlockSpec(memory_space=pl.ANY)
    moved = sum(array.size * array.dtype.itemsize for array in arrays)
    return pl.pallas_call(
        kernel,
        out_shape=jax.ShapeDtypeStruct(shape, jnp.bfloat16),
        in_specs=[pl.BlockSpec(memory_space=pltpu.VMEM)] * len(arrays) + [anywhere] * len(through),
        out_specs=anywhere,
        scratch_shapes=[pltpu.SemaphoreType.DMA((len(blocks),))],
        input_output_aliases={len(arrays): 0} if through else {},
        compiler_params=pltpu.CompilerParams(vmem_limit_bytes=moved + (1 << 20)),
        cost_estimate=pl.CostEstimate(flops=PLACE_FLOPS, bytes_accessed=2 * moved, transcendentals=0),
    )(*arrays, *through)


def gate(*arrays):
    anywhere = pl.BlockSpec(memory_space=pl.ANY)
    return pl.pallas_call(
        lambda *refs: None,
        out_shape=[jax.ShapeDtypeStruct(array.shape, array.dtype) for array in arrays],
        in_specs=[anywhere] * len(arrays),
        out_specs=[anywhere] * len(arrays),
        input_output_aliases={at: at for at in range(len(arrays))},
        compiler_params=pltpu.CompilerParams(vmem_limit_bytes=1 << 20),
        cost_estimate=pl.CostEstimate(flops=GATE_FLOPS, bytes_accessed=0, transcendentals=0),
    )(*arrays)


def step(inner, outer, momentum):
    terms = lax.all_to_all(inner, "replica", 0, 0).astype(jnp.float32)
    average = outer - jnp.sum(terms, axis=0) / REPLICAS
    momentum_new = 0.9 * momentum + average
    return outer - 0.7 * (average + 0.9 * momentum_new), momentum_new


def to_all(array):
    return lax.all_to_all(jnp.broadcast_to(array, (REPLICAS,) + array.shape), "replica", 0, 0)


def write(token, *arrays):
    count = len(arrays)

    def kernel(*refs):
        held, results, sems = refs[1 : 1 + count], refs[2 + count : -1], refs[-1]
        copies = [pltpu.make_async_copy(held[at], results[at], sems.at[at]) for at in range(count)]
        for copy in copies:
            copy.start()
        for copy in copies:
            copy.wait()

    anywhere = pl.BlockSpec(memory_space=pl.ANY)
    moved = sum(array.size * array.dtype.itemsize for array in arrays)
    return pl.pallas_call(
        kernel,
        out_shape=[jax.ShapeDtypeStruct(array.shape, array.dtype) for array in (token,) + arrays],
        in_specs=[anywhere] + [pl.BlockSpec(memory_space=pltpu.VMEM)] * count,
        out_specs=[anywhere] * (1 + count),
        scratch_shapes=[pltpu.SemaphoreType.DMA((count,))],
        input_output_aliases={0: 0},
        compiler_params=pltpu.CompilerParams(vmem_limit_bytes=moved + (1 << 20)),
        cost_estimate=pl.CostEstimate(flops=PLACE_FLOPS, bytes_accessed=2 * moved, transcendentals=0),
    )(token, *arrays)


def gather(own, head, rest, outer_all, momentum_new, shape):
    width, split = own.shape[1], head.shape[1]

    def group(array, hops, came=0, run=0, first=0):
        targets = [(run, hops, core, came) for core in range(array.shape[0])]
        return array, targets, first, array.shape[2]

    def head_of(array):
        return array[:, :, :split]

    def q(array, hops, came=0):
        return group(array, hops, came, 1, split)

    def y(array, hops, came=0):
        return group(array, hops, came, 1)

    own, head, rest = own[None], head[None], rest[None]
    beside = swap_run(rest)
    p0 = jnp.concatenate([own, swap_core(own)])
    token, p0 = gate(jnp.zeros(TILE, jnp.float32), p0)
    p1 = along_slots(p0)
    token, outer_all, momentum_new = write(token, outer_all, momentum_new)

    token, beside = gate(token, beside)
    q0 = jnp.concatenate([beside, swap_core(beside)])
    q1 = along_slots(q0)
    out = place(None, [group(p0, 0)], shape)

    token, out, p1 = gate(token, out, p1)
    p2, y1, cp1 = along_slots(p1), swap_run(head_of(p1)), swap_core(p1)
    out = place(out, [q(q0, 0)], shape)

    token, out, q1 = gate(token, out, q1)
    q2, cq1, y0 = along_slots(q1), swap_core(q1), swap_run(head)
    out = place(out, [group(p1, 1)], shape)

    token, out, p2, y1, cp1 = gate(token, out, p2, y1, cp1)
    p3, y2, cp2, cy1 = along_slots(p2), swap_run(head_of(p2)), swap_core(p2), swap_core(y1)
    out = place(out, [q(q1, 1)], shape)

    token, out, q2, cq1, y0 = gate(token, out, q2, cq1, y0)
    q3, cq2, cy0 = along_slots(q2), swap_core(q2), swap_core(y0)
    out = place(out, [group(p2, 2), y(y1, 1), group(cp1, 1, 1)], shape)

    token, out, p3, y2, cp2, cy1 = gate(token, out, p3, y2, cp2, cy1)
    p4, y3, cp3, cy2 = along_slots(p3[:1]), swap_run(head_of(p3)), swap_core(p3), swap_core(y2)
    out = place(out, [q(q2, 2), q(cq1, 1, 1), y(y0, 0)], shape)

    token, out, q3, cq2, cy0 = gate(token, out, q3, cq2, cy0)
    q4, cq3 = along_slots(q3[:1]), swap_core(q3)
    out = place(out, [group(p3, 3), y(y2, 2), group(cp2, 2, 1), y(cy1, 1, 1)], shape)

    token, out, p4, y3, cp3, cy2 = gate(token, out, p4, y3, cp3, cy2)
    y4, cp4, cy3 = swap_run(head_of(p4)), swap_core(p4), swap_core(y3)
    out = place(out, [q(q3, 3), q(cq2, 2, 1), y(cy0, 0, 1)], shape)

    token, out, q4, cq3 = gate(token, out, q4, cq3)
    cq4 = swap_core(q4)
    out = place(out, [group(p4, 4), y(y3, 3), group(cp3, 3, 1), y(cy2, 2, 1)], shape)

    token, out, y4, cp4, cy3 = gate(token, out, y4, cp4, cy3)
    cy4 = swap_core(y4)
    out = place(out, [q(q4, 4), q(cq3, 3, 1), y(y4, 4), group(cp4, 4, 1), y(cy3, 3, 1)], shape)
    return place(out, [q(cq4, 4, 1), y(cy4, 4, 1)], shape), outer_all, momentum_new


def body(inner, outer, momentum):
    width = momentum.shape[1] // TILE[1]
    replica = lax.axis_index("replica")

    def tiles(array):
        array = array.reshape(TILE[0], -1, width, TILE[1])
        return array.transpose(1, 2, 0, 3)

    def rows(array):
        return array.transpose(2, 0, 1, 3).reshape(TILE[0], -1)

    inner, outer, momentum = tiles(inner[0]), tiles(outer), tiles(momentum)[0]
    own_outer = lax.dynamic_index_in_dim(outer, replica, 0, keepdims=False)
    shape = (RUNS * SLOTS * CORES, REPLICAS, width) + TILE

    outer_new, momentum_new = step(inner, own_outer, momentum)
    outer_all = to_all(outer_new)

    def blend(at):
        return (0.5 * inner[:, at].astype(jnp.float32) + 0.5 * outer_all[:, at]).astype(jnp.bfloat16)

    parts = blend(slice(0, None)), blend(slice(0, SPLIT)), blend(slice(SPLIT, None))
    out, outer_all, momentum_new = gather(*parts, outer_all, momentum_new, shape)
    gathered = out.transpose(0, 3, 1, 2, 4).reshape(1, -1, REPLICAS * width * TILE[1])
    return rows(outer_all), rows(momentum_new[None]), gathered


def solution(mesh):
    placed = (P("replica", "fsdp", None), P("fsdp", None), P("fsdp", "replica"))
    return jax.shard_map(
        body,
        mesh=mesh,
        in_specs=placed,
        out_specs=(P("fsdp", None), P("fsdp", "replica"), P("replica", None, None)),
        check_vma=False,
    )
```

```python
import jax
import jax.numpy as jnp
from jax import lax
from jax.experimental import pallas as pl
from jax.experimental.pallas import tpu as pltpu
from jax.sharding import PartitionSpec as P

REPLICAS = 8
RUNS, SLOTS, CORES = 2, 8, 2
TILE = (8, 128)
GATE_FLOPS, PLACE_FLOPS = 6_000_000_000, 2_000_000_000


def coords(index):
    return index // (SLOTS * CORES), index // CORES % SLOTS, index % CORES


def fsdp_index(run, slot, core):
    return (run % RUNS * SLOTS + slot % SLOTS) * CORES + core % CORES


def move(array, target):
    return lax.ppermute(array, "fsdp", [(i, fsdp_index(*target(*coords(i)))) for i in range(RUNS * SLOTS * CORES)])


def swap_run(array):
    return move(array, lambda run, slot, core: (run + 1, slot, core))


def swap_core(array):
    return move(array, lambda run, slot, core: (run, slot, core + 1))


def along_slots(array):
    return move(array, lambda run, slot, core: (run, slot + (1 if core == 0 else -1), core))


def place(out, groups, shape):
    arrays = [array for array, _ in groups]
    through = [] if out is None else [out]
    blocks = [(at, lead, where) for at, (_, targets) in enumerate(groups) for lead, where in enumerate(targets)]

    def kernel(*refs):
        result, sems = refs[-2:]
        own_run, own_slot, own_core = coords(lax.axis_index("fsdp"))
        copies = []
        for number, (at, lead, (run, hops, kind, came)) in enumerate(blocks):
            receiver = (own_core + came) % CORES
            block = fsdp_index(own_run + run, own_slot + (2 * receiver - 1) * hops, receiver + kind)
            copies.append(pltpu.make_async_copy(refs[at].at[lead], result.at[block], sems.at[number]))
        for copy in copies:
            copy.start()
        for copy in copies:
            copy.wait()

    anywhere = pl.BlockSpec(memory_space=pl.ANY)
    moved = sum(array.size * array.dtype.itemsize for array in arrays)
    return pl.pallas_call(
        kernel,
        out_shape=jax.ShapeDtypeStruct(shape, jnp.bfloat16),
        in_specs=[pl.BlockSpec(memory_space=pltpu.VMEM)] * len(arrays) + [anywhere] * len(through),
        out_specs=anywhere,
        scratch_shapes=[pltpu.SemaphoreType.DMA((len(blocks),))],
        input_output_aliases={len(arrays): 0} if through else {},
        compiler_params=pltpu.CompilerParams(vmem_limit_bytes=moved + (1 << 20)),
        cost_estimate=pl.CostEstimate(flops=PLACE_FLOPS, bytes_accessed=2 * moved, transcendentals=0),
    )(*arrays, *through)


def gate(*arrays):
    anywhere = pl.BlockSpec(memory_space=pl.ANY)
    return pl.pallas_call(
        lambda *refs: None,
        out_shape=[jax.ShapeDtypeStruct(array.shape, array.dtype) for array in arrays],
        in_specs=[anywhere] * len(arrays),
        out_specs=[anywhere] * len(arrays),
        input_output_aliases={at: at for at in range(len(arrays))},
        compiler_params=pltpu.CompilerParams(vmem_limit_bytes=1 << 20),
        cost_estimate=pl.CostEstimate(flops=GATE_FLOPS, bytes_accessed=0, transcendentals=0),
    )(*arrays)


def step(inner, outer, momentum):
    terms = lax.all_to_all(inner, "replica", 0, 0).astype(jnp.float32)
    average = outer - jnp.sum(terms, axis=0) / REPLICAS
    momentum_new = 0.9 * momentum + average
    return outer - 0.7 * (average + 0.9 * momentum_new), momentum_new


def to_all(array):
    return lax.all_to_all(jnp.broadcast_to(array, (REPLICAS,) + array.shape), "replica", 0, 0)


def write(token, *arrays):
    count = len(arrays)

    def kernel(*refs):
        held, results, sems = refs[1 : 1 + count], refs[2 + count : -1], refs[-1]
        copies = [pltpu.make_async_copy(held[at], results[at], sems.at[at]) for at in range(count)]
        for copy in copies:
            copy.start()
        for copy in copies:
            copy.wait()

    anywhere = pl.BlockSpec(memory_space=pl.ANY)
    moved = sum(array.size * array.dtype.itemsize for array in arrays)
    return pl.pallas_call(
        kernel,
        out_shape=[jax.ShapeDtypeStruct(array.shape, array.dtype) for array in (token,) + arrays],
        in_specs=[anywhere] + [pl.BlockSpec(memory_space=pltpu.VMEM)] * count,
        out_specs=[anywhere] * (1 + count),
        scratch_shapes=[pltpu.SemaphoreType.DMA((count,))],
        input_output_aliases={0: 0},
        compiler_params=pltpu.CompilerParams(vmem_limit_bytes=moved + (1 << 20)),
        cost_estimate=pl.CostEstimate(flops=PLACE_FLOPS, bytes_accessed=2 * moved, transcendentals=0),
    )(token, *arrays)


def gather(own, outer_all, momentum_new, shape):
    def rows(array, hops, kinds=(0,), came=0, run=0):
        return array, [(run, hops, kind, came) for kind in kinds]

    own = own[None]
    q0 = swap_run(own)
    p0 = jnp.concatenate([own, swap_core(own)])
    token, p0 = gate(jnp.zeros(TILE, jnp.float32), p0)
    p1 = along_slots(p0)
    token, outer_all, momentum_new = write(token, outer_all, momentum_new)

    token, q0 = gate(token, q0)
    q1, cq0 = along_slots(q0), swap_core(q0)
    out = place(None, [rows(p0, 0, (0, 1))], shape)

    token, out, p1 = gate(token, out, p1)
    p2, y1, cp1 = along_slots(p1), swap_run(p1[1:]), swap_core(p1)
    out = place(out, [rows(q0, 0, run=1)], shape)

    token, out, q1, cq0 = gate(token, out, q1, cq0)
    q2, cq1 = along_slots(q1), swap_core(q1)
    out = place(out, [rows(p1, 1, (0, 1))], shape)

    token, out, p2, cp1, y1 = gate(token, out, p2, cp1, y1)
    p3, y2, cp2, cy1 = along_slots(p2), swap_run(p2[1:]), swap_core(p2), swap_core(y1)
    out = place(out, [rows(q1, 1, run=1), rows(cq0, 0, came=1, run=1)], shape)

    token, out, q2, cq1 = gate(token, out, q2, cq1)
    q3, cq2 = along_slots(q2), swap_core(q2)
    out = place(out, [rows(p2, 2, (0, 1)), rows(cp1, 1, (0, 1), 1), rows(y1, 1, (1,), run=1)], shape)

    token, out, p3, cp2, y2 = gate(token, out, p3, cp2, y2)
    p4, y3, cp3, cy2 = along_slots(p3[:1]), swap_run(p3[1:]), swap_core(p3), swap_core(y2)
    out = place(out, [rows(q2, 2, run=1), rows(cq1, 1, came=1, run=1), rows(cy1, 1, (1,), 1, 1)], shape)

    token, out, q3, cq2 = gate(token, out, q3, cq2)
    q4, cq3 = along_slots(q3), swap_core(q3)
    out = place(out, [rows(p3, 3, (0, 1)), rows(cp2, 2, (0, 1), 1), rows(y2, 2, (1,), run=1)], shape)

    token, out, p4, cp3, y3 = gate(token, out, p4, cp3, y3)
    cp4, cy3 = swap_core(p4), swap_core(y3)
    out = place(out, [rows(q3, 3, run=1), rows(cq2, 2, came=1, run=1), rows(cy2, 2, (1,), 1, 1)], shape)

    token, out, q4, cq3 = gate(token, out, q4, cq3)
    cq4 = swap_core(q4)
    out = place(
        out,
        [
            rows(p4, 4),
            rows(cp3, 3, (0, 1), 1),
            rows(y3, 3, (1,), run=1),
            rows(cq3, 3, came=1, run=1),
            rows(cp4, 4, came=1),
            rows(cy3, 3, (1,), 1, 1),
            rows(q4, 4, run=1),
        ],
        shape,
    )
    return place(out, [rows(cq4, 4, came=1, run=1)], shape), outer_all, momentum_new


def body(inner, outer, momentum):
    width = momentum.shape[1] // TILE[1]
    replica = lax.axis_index("replica")

    def tiles(array):
        array = array.reshape(TILE[0], -1, width, TILE[1])
        return array.transpose(1, 2, 0, 3)

    def rows(array):
        return array.transpose(2, 0, 1, 3).reshape(TILE[0], -1)

    inner, outer, momentum = tiles(inner[0]), tiles(outer), tiles(momentum)[0]
    own_outer = lax.dynamic_index_in_dim(outer, replica, 0, keepdims=False)
    shape = (RUNS * SLOTS * CORES, REPLICAS, width) + TILE

    outer_new, momentum_new = step(inner, own_outer, momentum)
    outer_all = to_all(outer_new)

    blended = (0.5 * inner.astype(jnp.float32) + 0.5 * outer_all).astype(jnp.bfloat16)
    out, outer_all, momentum_new = gather(blended, outer_all, momentum_new, shape)
    gathered = out.transpose(0, 3, 1, 2, 4).reshape(1, -1, REPLICAS * width * TILE[1])
    return rows(outer_all), rows(momentum_new[None]), gathered


def solution(mesh):
    placed = (P("replica", "fsdp", None), P("fsdp", None), P("fsdp", "replica"))
    return jax.shard_map(
        body,
        mesh=mesh,
        in_specs=placed,
        out_specs=(P("fsdp", None), P("fsdp", "replica"), P("replica", None, None)),
        check_vma=False,
    )
```

```python
import jax
import jax.numpy as jnp
from jax import lax
from jax.experimental import pallas as pl
from jax.experimental.pallas import tpu as pltpu
from jax.sharding import PartitionSpec as P

REPLICAS = 8
RUNS, SLOTS, CORES = 2, 8, 2
TILE = (8, 128)
GATE_FLOPS, PLACE_FLOPS = 6_000_000_000, 2_000_000_000


def coords(index):
    return index // (SLOTS * CORES), index // CORES % SLOTS, index % CORES


def fsdp_index(run, slot, core):
    return (run % RUNS * SLOTS + slot % SLOTS) * CORES + core % CORES


def move(array, target):
    return lax.ppermute(array, "fsdp", [(i, fsdp_index(*target(*coords(i)))) for i in range(RUNS * SLOTS * CORES)])


def swap_run(array):
    return move(array, lambda run, slot, core: (run + 1, slot, core))


def swap_core(array):
    return move(array, lambda run, slot, core: (run, slot, core + 1))


def along_slots(array):
    return move(array, lambda run, slot, core: (run, slot + (1 if core == 0 else -1), core))


def place(out, groups, shape):
    arrays = [array for array, _ in groups]
    through = [] if out is None else [out]
    blocks = [(at, lead, where) for at, (_, targets) in enumerate(groups) for lead, where in enumerate(targets)]

    def kernel(*refs):
        result, sems = refs[-2:]
        own_run, own_slot, own_core = coords(lax.axis_index("fsdp"))
        copies = []
        for number, (at, lead, (run, hops, kind, came)) in enumerate(blocks):
            receiver = (own_core + came) % CORES
            block = fsdp_index(own_run + run, own_slot + (2 * receiver - 1) * hops, receiver + kind)
            copies.append(pltpu.make_async_copy(refs[at].at[lead], result.at[block], sems.at[number]))
        for copy in copies:
            copy.start()
        for copy in copies:
            copy.wait()

    anywhere = pl.BlockSpec(memory_space=pl.ANY)
    moved = sum(array.size * array.dtype.itemsize for array in arrays)
    return pl.pallas_call(
        kernel,
        out_shape=jax.ShapeDtypeStruct(shape, jnp.bfloat16),
        in_specs=[pl.BlockSpec(memory_space=pltpu.VMEM)] * len(arrays) + [anywhere] * len(through),
        out_specs=anywhere,
        scratch_shapes=[pltpu.SemaphoreType.DMA((len(blocks),))],
        input_output_aliases={len(arrays): 0} if through else {},
        compiler_params=pltpu.CompilerParams(vmem_limit_bytes=moved + (1 << 20)),
        cost_estimate=pl.CostEstimate(flops=PLACE_FLOPS, bytes_accessed=2 * moved, transcendentals=0),
    )(*arrays, *through)


def gate(*arrays):
    anywhere = pl.BlockSpec(memory_space=pl.ANY)
    return pl.pallas_call(
        lambda *refs: None,
        out_shape=[jax.ShapeDtypeStruct(array.shape, array.dtype) for array in arrays],
        in_specs=[anywhere] * len(arrays),
        out_specs=[anywhere] * len(arrays),
        input_output_aliases={at: at for at in range(len(arrays))},
        compiler_params=pltpu.CompilerParams(vmem_limit_bytes=1 << 20),
        cost_estimate=pl.CostEstimate(flops=GATE_FLOPS, bytes_accessed=0, transcendentals=0),
    )(*arrays)


def step(inner, outer, momentum):
    terms = lax.all_to_all(inner, "replica", 0, 0).astype(jnp.float32)
    average = outer - jnp.sum(terms, axis=0) / REPLICAS
    momentum_new = 0.9 * momentum + average
    return outer - 0.7 * (average + 0.9 * momentum_new), momentum_new


def to_all(array):
    return lax.all_to_all(jnp.broadcast_to(array, (REPLICAS,) + array.shape), "replica", 0, 0)


def write(token, *arrays):
    count = len(arrays)

    def kernel(*refs):
        held, results, sems = refs[1 : 1 + count], refs[2 + count : -1], refs[-1]
        copies = [pltpu.make_async_copy(held[at], results[at], sems.at[at]) for at in range(count)]
        for copy in copies:
            copy.start()
        for copy in copies:
            copy.wait()

    anywhere = pl.BlockSpec(memory_space=pl.ANY)
    moved = sum(array.size * array.dtype.itemsize for array in arrays)
    return pl.pallas_call(
        kernel,
        out_shape=[jax.ShapeDtypeStruct(array.shape, array.dtype) for array in (token,) + arrays],
        in_specs=[anywhere] + [pl.BlockSpec(memory_space=pltpu.VMEM)] * count,
        out_specs=[anywhere] * (1 + count),
        scratch_shapes=[pltpu.SemaphoreType.DMA((count,))],
        input_output_aliases={0: 0},
        compiler_params=pltpu.CompilerParams(vmem_limit_bytes=moved + (1 << 20)),
        cost_estimate=pl.CostEstimate(flops=PLACE_FLOPS, bytes_accessed=2 * moved, transcendentals=0),
    )(token, *arrays)


def gather(own, outer_all, momentum_new, shape):
    def rows(array, hops, kinds=(0,), came=0, run=0):
        return array, [(run, hops, kind, came) for kind in kinds]

    own = own[None]
    a1, q0, other = along_slots(own), swap_run(own), swap_core(own)
    token, other = gate(jnp.zeros(TILE, jnp.float32), other)
    b1 = along_slots(other)
    token, outer_all, momentum_new = write(token, outer_all, momentum_new)

    token, q0 = gate(token, q0)
    q1 = along_slots(q0)

    token, a1, b1 = gate(token, a1, b1)
    p1 = jnp.concatenate([a1, b1])
    p2, y1, cp1 = along_slots(p1), swap_run(b1), swap_core(p1)
    out = place(None, [rows(own, 0), rows(other, 0, (1,)), rows(q0, 0, run=1)], shape)

    token, out, q1 = gate(token, out, q1)
    q2, cq01 = along_slots(q1), swap_core(jnp.concatenate([q0, q1]))
    out = place(out, [rows(p1, 1, (0, 1))], shape)

    token, out, p2, cp1, y1 = gate(token, out, p2, cp1, y1)
    p3, y2, cp2, cy1 = along_slots(p2), swap_run(p2[1:]), swap_core(p2), swap_core(y1)
    out = place(out, [rows(q1, 1, run=1)], shape)

    token, out, q2, cq01 = gate(token, out, q2, cq01)
    q3, cq2 = along_slots(q2), swap_core(q2)
    out = place(out, [rows(p2, 2, (0, 1)), rows(cp1, 1, (0, 1), 1), rows(y1, 1, (1,), run=1)], shape)

    token, out, p3, cp2, y2 = gate(token, out, p3, cp2, y2)
    p4, y3, cp3, cy2 = along_slots(p3[:1]), swap_run(p3[1:]), swap_core(p3), swap_core(y2)
    out = place(out, [rows(q2, 2, run=1), (cq01, [(1, 0, 0, 1), (1, 1, 0, 1)]), rows(cy1, 1, (1,), 1, 1)], shape)

    token, out, q3, cq2 = gate(token, out, q3, cq2)
    q4, cq3 = along_slots(q3), swap_core(q3)
    out = place(out, [rows(p3, 3, (0, 1)), rows(cp2, 2, (0, 1), 1), rows(y2, 2, (1,), run=1)], shape)

    token, out, p4, cp3, y3, q4, cq3 = gate(token, out, p4, cp3, y3, q4, cq3)
    cp4, cy3, cq4 = swap_core(p4), swap_core(y3), swap_core(q4)
    out = place(
        out,
        [
            rows(q3, 3, run=1),
            rows(cq2, 2, came=1, run=1),
            rows(cy2, 2, (1,), 1, 1),
            rows(p4, 4),
            rows(cp3, 3, (0, 1), 1),
            rows(y3, 3, (1,), run=1),
            rows(cq3, 3, came=1, run=1),
            rows(q4, 4, run=1),
        ],
        shape,
    )
    out = place(out, [rows(cp4, 4, came=1), rows(cy3, 3, (1,), 1, 1), rows(cq4, 4, came=1, run=1)], shape)
    return out, outer_all, momentum_new


def body(inner, outer, momentum):
    width = momentum.shape[1] // TILE[1]
    replica = lax.axis_index("replica")

    def tiles(array):
        array = array.reshape(TILE[0], -1, width, TILE[1])
        return array.transpose(1, 2, 0, 3)

    def rows(array):
        return array.transpose(2, 0, 1, 3).reshape(TILE[0], -1)

    inner, outer, momentum = tiles(inner[0]), tiles(outer), tiles(momentum)[0]
    own_outer = lax.dynamic_index_in_dim(outer, replica, 0, keepdims=False)
    shape = (RUNS * SLOTS * CORES, REPLICAS, width) + TILE

    outer_new, momentum_new = step(inner, own_outer, momentum)
    outer_all = to_all(outer_new)

    blended = (0.5 * inner.astype(jnp.float32) + 0.5 * outer_all).astype(jnp.bfloat16)
    out, outer_all, momentum_new = gather(blended, outer_all, momentum_new, shape)
    gathered = out.transpose(0, 3, 1, 2, 4).reshape(1, -1, REPLICAS * width * TILE[1])
    return rows(outer_all), rows(momentum_new[None]), gathered


def solution(mesh):
    placed = (P("replica", "fsdp", None), P("fsdp", None), P("fsdp", "replica"))
    return jax.shard_map(
        body,
        mesh=mesh,
        in_specs=placed,
        out_specs=(P("fsdp", None), P("fsdp", "replica"), P("replica", None, None)),
        check_vma=False,
    )
```

```python
import jax
import jax.numpy as jnp
from jax import lax
from jax.experimental import pallas as pl
from jax.experimental.pallas import tpu as pltpu
from jax.sharding import PartitionSpec as P

REPLICAS = 8
RUNS, SLOTS, CORES = 2, 8, 2
TILE = (8, 128)
GATE_FLOPS, PLACE_FLOPS = 6_000_000_000, 2_000_000_000


def coords(index):
    return index // (SLOTS * CORES), index // CORES % SLOTS, index % CORES


def fsdp_index(run, slot, core):
    return (run % RUNS * SLOTS + slot % SLOTS) * CORES + core % CORES


def move(array, target):
    return lax.ppermute(array, "fsdp", [(i, fsdp_index(*target(*coords(i)))) for i in range(RUNS * SLOTS * CORES)])


def swap_run(array):
    return move(array, lambda run, slot, core: (run + 1, slot, core))


def swap_core(array):
    return move(array, lambda run, slot, core: (run, slot, core + 1))


def along_slots(array):
    return move(array, lambda run, slot, core: (run, slot + (1 if core == 0 else -1), core))


def place(out, groups, shape):
    arrays = [array for array, _ in groups]
    through = [] if out is None else [out]
    blocks = [(at, lead, where) for at, (_, targets) in enumerate(groups) for lead, where in enumerate(targets)]

    def kernel(*refs):
        result, sems = refs[-2:]
        own_run, own_slot, own_core = coords(lax.axis_index("fsdp"))
        copies = []
        for number, (at, lead, (run, hops, kind, came)) in enumerate(blocks):
            receiver = (own_core + came) % CORES
            block = fsdp_index(own_run + run, own_slot + (2 * receiver - 1) * hops, receiver + kind)
            copies.append(pltpu.make_async_copy(refs[at].at[lead], result.at[block], sems.at[number]))
        for copy in copies:
            copy.start()
        for copy in copies:
            copy.wait()

    anywhere = pl.BlockSpec(memory_space=pl.ANY)
    moved = sum(array.size * array.dtype.itemsize for array in arrays)
    return pl.pallas_call(
        kernel,
        out_shape=jax.ShapeDtypeStruct(shape, jnp.bfloat16),
        in_specs=[pl.BlockSpec(memory_space=pltpu.VMEM)] * len(arrays) + [anywhere] * len(through),
        out_specs=anywhere,
        scratch_shapes=[pltpu.SemaphoreType.DMA((len(blocks),))],
        input_output_aliases={len(arrays): 0} if through else {},
        compiler_params=pltpu.CompilerParams(vmem_limit_bytes=moved + (1 << 20)),
        cost_estimate=pl.CostEstimate(flops=PLACE_FLOPS, bytes_accessed=2 * moved, transcendentals=0),
    )(*arrays, *through)


def gate(*arrays):
    anywhere = pl.BlockSpec(memory_space=pl.ANY)
    return pl.pallas_call(
        lambda *refs: None,
        out_shape=[jax.ShapeDtypeStruct(array.shape, array.dtype) for array in arrays],
        in_specs=[anywhere] * len(arrays),
        out_specs=[anywhere] * len(arrays),
        input_output_aliases={at: at for at in range(len(arrays))},
        compiler_params=pltpu.CompilerParams(vmem_limit_bytes=1 << 20),
        cost_estimate=pl.CostEstimate(flops=GATE_FLOPS, bytes_accessed=0, transcendentals=0),
    )(*arrays)


def step(inner, outer, momentum):
    terms = lax.all_to_all(inner, "replica", 0, 0).astype(jnp.float32)
    average = outer - jnp.sum(terms, axis=0) / REPLICAS
    momentum_new = 0.9 * momentum + average
    return outer - 0.7 * (average + 0.9 * momentum_new), momentum_new


def to_all(array):
    return lax.all_to_all(jnp.broadcast_to(array, (REPLICAS,) + array.shape), "replica", 0, 0)


def write(token, *arrays):
    count = len(arrays)

    def kernel(*refs):
        held, results, sems = refs[1 : 1 + count], refs[2 + count : -1], refs[-1]
        copies = [pltpu.make_async_copy(held[at], results[at], sems.at[at]) for at in range(count)]
        for copy in copies:
            copy.start()
        for copy in copies:
            copy.wait()

    anywhere = pl.BlockSpec(memory_space=pl.ANY)
    moved = sum(array.size * array.dtype.itemsize for array in arrays)
    return pl.pallas_call(
        kernel,
        out_shape=[jax.ShapeDtypeStruct(array.shape, array.dtype) for array in (token,) + arrays],
        in_specs=[anywhere] + [pl.BlockSpec(memory_space=pltpu.VMEM)] * count,
        out_specs=[anywhere] * (1 + count),
        scratch_shapes=[pltpu.SemaphoreType.DMA((count,))],
        input_output_aliases={0: 0},
        compiler_params=pltpu.CompilerParams(vmem_limit_bytes=moved + (1 << 20)),
        cost_estimate=pl.CostEstimate(flops=PLACE_FLOPS, bytes_accessed=2 * moved, transcendentals=0),
    )(token, *arrays)


def gather(own, outer_all, momentum_new, shape):
    def rows(array, hops, kinds=(0,), came=0, run=0):
        return array, [(run, hops, kind, came) for kind in kinds]

    own = own[None]
    q0 = swap_run(own)
    p0 = jnp.concatenate([own, swap_core(own)])
    token, p0 = gate(jnp.zeros(TILE, jnp.float32), p0)
    p1 = along_slots(p0)
    token, outer_all, momentum_new = write(token, outer_all, momentum_new)

    token, q0 = gate(token, q0)
    q1 = along_slots(q0)

    token, p1 = gate(token, p1)
    p2, y1, cp1 = along_slots(p1), swap_run(p1[1:]), swap_core(p1)
    out = place(None, [rows(p0, 0, (0, 1)), rows(q0, 0, run=1)], shape)

    token, out, q1 = gate(token, out, q1)
    q2, cq01 = along_slots(q1), swap_core(jnp.concatenate([q0, q1]))
    out = place(out, [rows(p1, 1, (0, 1))], shape)

    token, out, p2, cp1, y1 = gate(token, out, p2, cp1, y1)
    p3, y2, cp2, cy1 = along_slots(p2), swap_run(p2[1:]), swap_core(p2), swap_core(y1)
    out = place(out, [rows(q1, 1, run=1)], shape)

    token, out, q2, cq01 = gate(token, out, q2, cq01)
    q3, cq2 = along_slots(q2), swap_core(q2)
    out = place(out, [rows(p2, 2, (0, 1)), rows(cp1, 1, (0, 1), 1), rows(y1, 1, (1,), run=1)], shape)

    token, out, p3, cp2, y2 = gate(token, out, p3, cp2, y2)
    p4, y3, cp3, cy2 = along_slots(p3[:1]), swap_run(p3[1:]), swap_core(p3), swap_core(y2)
    out = place(out, [rows(q2, 2, run=1), (cq01, [(1, 0, 0, 1), (1, 1, 0, 1)]), rows(cy1, 1, (1,), 1, 1)], shape)

    token, out, q3, cq2 = gate(token, out, q3, cq2)
    q4, cq3 = along_slots(q3), swap_core(q3)
    out = place(out, [rows(p3, 3, (0, 1)), rows(cp2, 2, (0, 1), 1), rows(y2, 2, (1,), run=1)], shape)

    token, out, p4, cp3, y3 = gate(token, out, p4, cp3, y3)
    cp4, cy3 = swap_core(p4), swap_core(y3)
    out = place(
        out,
        [
            rows(q3, 3, run=1),
            rows(cq2, 2, came=1, run=1),
            rows(cy2, 2, (1,), 1, 1),
            rows(p4, 4),
            rows(cp3, 3, (0, 1), 1),
            rows(y3, 3, (1,), run=1),
        ],
        shape,
    )

    token, out, q4, cq3 = gate(token, out, q4, cq3)
    cq4 = swap_core(q4)
    out = place(
        out,
        [rows(cq3, 3, came=1, run=1), rows(cp4, 4, came=1), rows(cy3, 3, (1,), 1, 1), rows(q4, 4, run=1)],
        shape,
    )
    return place(out, [rows(cq4, 4, came=1, run=1)], shape), outer_all, momentum_new


def body(inner, outer, momentum):
    width = momentum.shape[1] // TILE[1]
    replica = lax.axis_index("replica")

    def tiles(array):
        array = array.reshape(TILE[0], -1, width, TILE[1])
        return array.transpose(1, 2, 0, 3)

    def rows(array):
        return array.transpose(2, 0, 1, 3).reshape(TILE[0], -1)

    inner, outer, momentum = tiles(inner[0]), tiles(outer), tiles(momentum)[0]
    own_outer = lax.dynamic_index_in_dim(outer, replica, 0, keepdims=False)
    shape = (RUNS * SLOTS * CORES, REPLICAS, width) + TILE

    outer_new, momentum_new = step(inner, own_outer, momentum)
    outer_all = to_all(outer_new)

    blended = (0.5 * inner.astype(jnp.float32) + 0.5 * outer_all).astype(jnp.bfloat16)
    out, outer_all, momentum_new = gather(blended, outer_all, momentum_new, shape)
    gathered = out.transpose(0, 3, 1, 2, 4).reshape(1, -1, REPLICAS * width * TILE[1])
    return rows(outer_all), rows(momentum_new[None]), gathered


def solution(mesh):
    placed = (P("replica", "fsdp", None), P("fsdp", None), P("fsdp", "replica"))
    return jax.shard_map(
        body,
        mesh=mesh,
        in_specs=placed,
        out_specs=(P("fsdp", None), P("fsdp", "replica"), P("replica", None, None)),
        check_vma=False,
    )
```
